32 devices in a mesh: ctx: 4 (over z), chan: 8 (over y, x, core).
Axes of the slice: x: 2, y: 2, z: 4, core: 2. Of those that a mesh axis runs over, the one named last changes fastest.
Arguments:
- value: bfloat16 [64, 16384], P('chan', 'ctx'), may hold values from -6 to 6
- gate: bfloat16 [64, 16384], P('chan', 'ctx'), may hold values from -6 to 6
- residual: float32 [64, 16384], P('chan', 'ctx'), may hold values from -24 to 24
- rates: float32 [64, 16], P('chan'), may hold values from 3.0517578e-05 to 0.05
- residues: float32 [64, 16], P('chan'), may hold values from -1.5 to 1.5
- skip: float32 [64], P('chan'), may hold values from -3 to 3
- gain: float32 [64], P('chan'), may hold values from 0.5 to 1.5
Outputs:
- mixed: float32 [64, 16384], P('chan', 'ctx')
- normed: bfloat16 [64, 16384], P('chan', 'ctx')
The draws below stay inside these ranges and needn't reach their ends.
All inputs are finite; a program needn't handle non-finite values.
Results may differ from the reference program's by a relative error of at most 0.0004.
Values may be sent and summed in bfloat16 or wider, within the bound.
A program may use at most 128 MiB of HBM per device.

```python
import math
import jax
import jax.numpy as jnp
from jax import lax

MODES = 16
CHANNELS = 64
TOKENS = 16384


def draw_residual(key, part):
    key = jax.random.fold_in(key, 7)
    key_a, key_b, key_c = jax.random.split(key, 3)
    ramp = jnp.arange(CHANNELS).astype(jnp.float32) / max(CHANNELS - 1, 1)
    column = jnp.exp(jax.random.uniform(key_b, (CHANNELS, 1), jnp.float32, jnp.log(0.3), 0.0)) * jnp.exp(ramp * jnp.log(3.0))[:, None]
    row = jnp.exp(jax.random.uniform(key_c, (1, TOKENS), jnp.float32, jnp.log(0.5), jnp.log(1.6)))
    entries = jnp.clip(jax.random.normal(key_a, (CHANNELS, TOKENS), jnp.float32), -4.0, 4.0)
    return (entries * column * row).astype(jnp.float32)


def shard_levels(key, extent, shards, least, top_value):
    def one(axis_at, shards_of):
        steps = jax.random.uniform(jax.random.fold_in(jax.random.fold_in(key, 6), axis_at), (shards_of,), jnp.float32, least / len(shards), top_value / len(shards))
        return jnp.repeat(jnp.exp(steps), extent[axis_at] // shards_of).reshape((-1,) + (1,) * (len(extent) - axis_at - 1))

    factor_of = one(*shards[0])
    for cut in shards[1:]:
        factor_of = factor_of * one(*cut)
    return factor_of


def centred(key, shape, spread, reach, shards=(), dtype=jnp.bfloat16):
    array = jax.random.normal(key, shape, jnp.float32) * spread
    if len(shards) > 0:
        array = shard_levels(key, shape, shards, -0.22, 0.18) * array
    return jnp.clip(array, min=-reach, max=reach).astype(dtype)


def setup_inputs(seed: int = 0) -> dict:
    seeds = jax.random.split(jax.random.key(seed), 8)
    value = centred(seeds[0], (CHANNELS, TOKENS), 1.0, 6.0, ((0, 8), (1, 4)))
    gate = centred(seeds[1], (CHANNELS, TOKENS), 1.0, 6.0, ((0, 8), (1, 4)))
    residual = draw_residual(jax.random.fold_in(seeds[7], 71), 0)
    rates = jnp.clip(jnp.exp(math.log(0.05) - 7.4014754 * jax.random.uniform(seeds[3], (CHANNELS, MODES), jnp.float32) ** shard_levels(seeds[3], (CHANNELS, MODES), ((0, 8),), -0.2, 0.2)), 3.0517578125e-05, 0.05)
    residues = centred(seeds[4], (CHANNELS, MODES), 0.25, 1.5, ((0, 8),), jnp.float32)
    skip = centred(seeds[5], (CHANNELS,), 0.5, 3.0, ((0, 8),), jnp.float32)
    gain = jnp.clip(1.0 + 0.1 * jax.random.normal(seeds[6], (CHANNELS,), jnp.float32), 0.5, 1.5)
    return dict(value=value, gate=gate, residual=residual, rates=rates, residues=residues, skip=skip, gain=gain)


def reference(value, gate, residual, rates, residues, skip, gain):
    times = jnp.arange(TOKENS).astype(jnp.float32)
    taps = jnp.zeros((CHANNELS, TOKENS), jnp.float32)
    for mode in range(MODES):
        rate = rates[:, mode:mode + 1]
        weight = residues[:, mode:mode + 1] * jnp.sqrt(2.0 * rate)
        taps = taps + weight * jnp.exp(-rate * times[None, :])
    signal = value.astype(jnp.float32)
    length = 2 * TOKENS
    spectrum = jnp.fft.rfft(signal, n=length, axis=1) * jnp.fft.rfft(taps, n=length, axis=1)
    conv = jnp.fft.irfft(spectrum, n=length, axis=1)[:, :TOKENS].astype(jnp.float32)
    conv = conv + skip[:, None] * signal
    mixed = residual + gate.astype(jnp.float32) * conv
    square_mean = lax.optimization_barrier(jnp.mean(mixed * mixed, axis=0))
    normed = (mixed * jax.lax.rsqrt(square_mean + 1e-06)[None, :] * gain[:, None]).astype(jnp.bfloat16)
    return (mixed, normed)
```

```python
import functools

import jax
import jax.numpy as jnp
from jax import lax
from jax.experimental import pallas as pl
from jax.experimental.pallas import tpu as pltpu
from jax.sharding import PartitionSpec as P

CHUNK = 128
F32 = jnp.float32
BF16 = jnp.bfloat16
MESH = pl.DeviceIdType.MESH


def two_terms(x):
    high = x.astype(BF16)
    return high, (x - high.astype(F32)).astype(BF16)


def stack_chunks(x, count):
    return jnp.concatenate([x[:, k * CHUNK:(k + 1) * CHUNK] for k in range(count)], axis=0)


def column_of(ref, count):
    row = lax.broadcasted_iota(jnp.int32, (count, CHUNK), 0)
    out = jnp.zeros((count, CHUNK), F32)
    for c in range(count):
        out = jnp.where(row == c, ref[c], out)
    return out


def kernel(
    n_ctx, n_chan,
    value_ref, gate_ref, residual_ref, rates_ref, residues_ref, skip_ref, gain_ref,
    mixed_ref, normed_ref,
    state_out, state_in, square_out, square_in,
    state_send, state_recv, square_send, square_recv,
):
    ctx = lax.axis_index("ctx")
    chan = lax.axis_index("chan")
    channels, local_len = value_ref.shape
    modes = rates_ref.shape[1]
    lanes = channels * modes
    count = local_len // CHUNK

    barrier = pltpu.get_barrier_semaphore()
    for step in range(1, n_ctx):
        pl.semaphore_signal(
            barrier, inc=1, device_id={"ctx": lax.rem(ctx + step, n_ctx)}, device_id_type=MESH
        )
    for step in range(1, n_chan):
        pl.semaphore_signal(
            barrier, inc=1, device_id={"chan": lax.rem(chan + step, n_chan)}, device_id_type=MESH
        )

    rates = rates_ref[...]
    weights = residues_ref[...] * jnp.sqrt(2.0 * rates)
    row8 = lax.broadcasted_iota(jnp.int32, (channels, lanes), 0)
    lane8 = lax.broadcasted_iota(jnp.int32, (channels, lanes), 1)
    token = lax.broadcasted_iota(jnp.int32, (channels, CHUNK), 1)
    time = token.astype(F32)
    taps = jnp.zeros((channels, CHUNK), F32)
    rate_rows = jnp.zeros((channels, lanes), F32)
    weight_rows = jnp.zeros((channels, lanes), F32)
    for m in range(modes):
        rate = jnp.broadcast_to(rates[:, m:m + 1], (channels, CHUNK))
        weight = jnp.broadcast_to(weights[:, m:m + 1], (channels, CHUNK))
        taps = taps + weight * jnp.exp(-rate * time)
        here = lane8 % modes == m
        rate_rows = jnp.where(here, rate, rate_rows)
        weight_rows = jnp.where(here, weight, weight_rows)
    own = row8 == lane8 // modes
    rate_lane = jnp.sum(jnp.where(own, rate_rows, 0.0), axis=0, keepdims=True)
    weight_lane = jnp.sum(jnp.where(own, weight_rows, 0.0), axis=0, keepdims=True)

    signal = stack_chunks(value_ref[...].astype(F32), count)
    signal16 = signal.astype(BF16)
    place = lax.broadcasted_iota(jnp.int32, (CHUNK, lanes), 0).astype(F32)
    enter = jnp.exp(-rate_lane * (CHUNK - 1.0 - place))
    enter2 = jnp.concatenate(two_terms(enter), axis=1)
    added = jnp.dot(signal16, enter2, preferred_element_type=F32)
    added = added[:, :lanes] + added[:, lanes:]
    chunk_decay = jnp.exp(-rate_lane * float(CHUNK))
    state = jnp.zeros((channels, lanes), F32)
    states = []
    for k in range(count):
        states.append(state)
        chunk = jnp.where(own, added[k * channels:(k + 1) * channels], 0.0)
        state = chunk_decay * state + chunk
    state_out[...] = state

    pl.semaphore_wait(barrier, n_ctx - 1 + n_chan - 1)
    state_copies = []
    for step in range(1, n_ctx):
        copy = pltpu.make_async_remote_copy(
            src_ref=state_out,
            dst_ref=state_in.at[step - 1],
            send_sem=state_send.at[step - 1],
            recv_sem=state_recv.at[step - 1],
            device_id={"ctx": lax.rem(ctx + step, n_ctx)},
            device_id_type=MESH,
        )
        copy.start()
        state_copies.append(copy)

    taps = taps + jnp.where(token == 0, column_of(skip_ref, channels), 0.0)
    target = lax.broadcasted_iota(jnp.int32, (CHUNK, CHUNK), 1)
    source = lax.broadcasted_iota(jnp.int32, (CHUNK, CHUNK), 0)
    channel_of = lax.broadcasted_iota(jnp.int32, (count * channels, CHUNK), 0) % channels
    left, right = [], []
    for c in range(channels):
        wide = jnp.broadcast_to(taps[c:c + 1], (CHUNK, CHUNK))
        turned = pltpu.roll(wide, 0, 1, stride=1, stride_axis=0)
        toeplitz = jnp.where(target >= source, turned, 0.0)
        right.append(jnp.concatenate(two_terms(toeplitz), axis=1))
        left.append(jnp.where(channel_of == c, signal, 0.0).astype(BF16))
    near = jnp.dot(
        jnp.concatenate(left, axis=1), jnp.concatenate(right, axis=0), preferred_element_type=F32
    )
    leave = weight_lane * jnp.exp(-rate_lane * (place + 1.0))
    leave2 = jnp.concatenate(two_terms(leave), axis=0)
    leave2 = jnp.concatenate([leave2, leave2], axis=1)
    power = jnp.exp(
        -rate_lane * (float(CHUNK) * lax.broadcasted_iota(jnp.int32, (count, lanes), 0).astype(F32))
    )

    carry = jnp.zeros((channels, lanes), F32)
    for step in range(1, n_ctx):
        state_copies[step - 1].wait()
        decay = jnp.exp(-rate_lane * float(local_len * (step - 1)))
        carry = carry + jnp.where(ctx >= step, decay, 0.0) * state_in[step - 1]
    full = jnp.concatenate([states[k] + power[k:k + 1] * carry for k in range(count)], axis=0)
    far = lax.dot_general(
        jnp.concatenate(two_terms(full), axis=1), leave2, (((1,), (1,)), ((), ())),
        preferred_element_type=F32,
    )
    both = near + far
    conv = both[:, :CHUNK] + both[:, CHUNK:]
    mixed = stack_chunks(residual_ref[...], count) + stack_chunks(gate_ref[...].astype(F32), count) * conv
    square_out[...] = jnp.sum((mixed * mixed).reshape(count, channels, CHUNK), axis=1)

    square_copies = []
    for step in range(1, n_chan):
        copy = pltpu.make_async_remote_copy(
            src_ref=square_out,
            dst_ref=square_in.at[step - 1],
            send_sem=square_send.at[step - 1],
            recv_sem=square_recv.at[step - 1],
            device_id={"chan": lax.rem(chan + step, n_chan)},
            device_id_type=MESH,
        )
        copy.start()
        square_copies.append(copy)
    gain = column_of(gain_ref, channels)
    for k in range(count):
        mixed_ref[:, k * CHUNK:(k + 1) * CHUNK] = mixed[k * channels:(k + 1) * channels]
    total = square_out[...]
    for step in range(1, n_chan):
        square_copies[step - 1].wait()
        total = total + square_in[step - 1]
    scale = lax.rsqrt(total / float(channels * n_chan) + 1e-06)
    for k in range(count):
        normed = mixed[k * channels:(k + 1) * channels] * scale[k:k + 1] * gain
        normed_ref[:, k * CHUNK:(k + 1) * CHUNK] = normed.astype(BF16)


def local(n_ctx, n_chan, value, gate, residual, rates, residues, skip, gain):
    channels, local_len = value.shape
    lanes = channels * rates.shape[1]
    count = local_len // CHUNK
    vmem = pl.BlockSpec(memory_space=pltpu.VMEM)
    smem = pl.BlockSpec(memory_space=pltpu.SMEM)
    return pl.pallas_call(
        functools.partial(kernel, n_ctx, n_chan),
        out_shape=(
            jax.ShapeDtypeStruct((channels, local_len), F32),
            jax.ShapeDtypeStruct((channels, local_len), BF16),
        ),
        in_specs=[vmem] * 5 + [smem] * 2,
        out_specs=(vmem, vmem),
        scratch_shapes=[
            pltpu.VMEM((channels, lanes), F32),
            pltpu.VMEM((n_ctx - 1, channels, lanes), F32),
            pltpu.VMEM((count, CHUNK), F32),
            pltpu.VMEM((n_chan - 1, count, CHUNK), F32),
            pltpu.SemaphoreType.DMA((n_ctx - 1,)),
            pltpu.SemaphoreType.DMA((n_ctx - 1,)),
            pltpu.SemaphoreType.DMA((n_chan - 1,)),
            pltpu.SemaphoreType.DMA((n_chan - 1,)),
        ],
        compiler_params=pltpu.CompilerParams(
            collective_id=0, has_side_effects=True, vmem_limit_bytes=32 * 1024 * 1024
        ),
        cost_estimate=pl.CostEstimate(
            flops=2 * count * channels * CHUNK * 2 * (channels * CHUNK + 3 * lanes),
            bytes_accessed=14 * channels * local_len,
            transcendentals=64 * 1024,
        ),
    )(value, gate, residual, rates, residues, skip, gain)


def solution(mesh):
    return jax.shard_map(
        functools.partial(local, mesh.shape["ctx"], mesh.shape["chan"]),
        mesh=mesh,
        in_specs=(
            P("chan", "ctx"),
            P("chan", "ctx"),
            P("chan", "ctx"),
            P("chan", None),
            P("chan", None),
            P("chan"),
            P("chan"),
        ),
        out_specs=(P("chan", "ctx"), P("chan", "ctx")),
        check_vma=False,
    )
```

```python
import functools

import jax
import jax.numpy as jnp
from jax import lax
from jax.experimental import pallas as pl
from jax.experimental.pallas import tpu as pltpu
from jax.sharding import PartitionSpec as P

CHUNK = 128
F32 = jnp.float32
BF16 = jnp.bfloat16
MESH = pl.DeviceIdType.MESH


def two_terms(x):
    high = x.astype(BF16)
    return high, (x - high.astype(F32)).astype(BF16)


def stack_chunks(x, count):
    return jnp.concatenate([x[:, k * CHUNK:(k + 1) * CHUNK] for k in range(count)], axis=0)


def column_of(ref, count):
    row = lax.broadcasted_iota(jnp.int32, (count, CHUNK), 0)
    out = jnp.zeros((count, CHUNK), F32)
    for c in range(count):
        out = jnp.where(row == c, ref[c], out)
    return out


def kernel(
    n_ctx, n_chan,
    value_hbm, gate_hbm, residual_hbm, rates_hbm, residues_hbm, skip_hbm, gain_hbm,
    mixed_ref, normed_ref,
    rates_ref, residues_ref, value_ref, skip_ref, residual_ref, gate_ref, gain_ref, load_sem,
    state_out, state_in, square_out, square_in,
    state_send, state_recv, square_send, square_recv,
):
    loads = {}
    for order, (name, source, target) in enumerate([
        ("rates", rates_hbm, rates_ref),
        ("residues", residues_hbm, residues_ref),
        ("value", value_hbm, value_ref),
        ("skip", skip_hbm, skip_ref),
        ("residual", residual_hbm, residual_ref),
        ("gate", gate_hbm, gate_ref),
        ("gain", gain_hbm, gain_ref),
    ]):
        loads[name] = pltpu.make_async_copy(source, target, load_sem.at[order])
        loads[name].start()
    ctx = lax.axis_index("ctx")
    chan = lax.axis_index("chan")
    channels, local_len = value_ref.shape
    modes = rates_ref.shape[1]
    lanes = channels * modes
    count = local_len // CHUNK

    barrier = pltpu.get_barrier_semaphore()
    for step in range(1, n_ctx):
        pl.semaphore_signal(
            barrier, inc=1, device_id={"ctx": lax.rem(ctx + step, n_ctx)}, device_id_type=MESH
        )
    for step in range(1, n_chan):
        pl.semaphore_signal(
            barrier, inc=1, device_id={"chan": lax.rem(chan + step, n_chan)}, device_id_type=MESH
        )

    loads["rates"].wait()
    loads["residues"].wait()
    rates = rates_ref[...]
    weights = residues_ref[...] * jnp.sqrt(2.0 * rates)
    row8 = lax.broadcasted_iota(jnp.int32, (channels, lanes), 0)
    lane8 = lax.broadcasted_iota(jnp.int32, (channels, lanes), 1)
    token = lax.broadcasted_iota(jnp.int32, (channels, CHUNK), 1)
    time = token.astype(F32)
    taps = jnp.zeros((channels, CHUNK), F32)
    rate_rows = jnp.zeros((channels, lanes), F32)
    weight_rows = jnp.zeros((channels, lanes), F32)
    for m in range(modes):
        rate = jnp.broadcast_to(rates[:, m:m + 1], (channels, CHUNK))
        weight = jnp.broadcast_to(weights[:, m:m + 1], (channels, CHUNK))
        taps = taps + weight * jnp.exp(-rate * time)
        here = lane8 % modes == m
        rate_rows = jnp.where(here, rate, rate_rows)
        weight_rows = jnp.where(here, weight, weight_rows)
    own = row8 == lane8 // modes
    rate_lane = jnp.sum(jnp.where(own, rate_rows, 0.0), axis=0, keepdims=True)
    weight_lane = jnp.sum(jnp.where(own, weight_rows, 0.0), axis=0, keepdims=True)

    loads["value"].wait()
    signal = stack_chunks(value_ref[...].astype(F32), count)
    signal16 = signal.astype(BF16)
    place = lax.broadcasted_iota(jnp.int32, (CHUNK, lanes), 0).astype(F32)
    enter = jnp.exp(-rate_lane * (CHUNK - 1.0 - place))
    enter2 = jnp.concatenate(two_terms(enter), axis=1)
    added = jnp.dot(signal16, enter2, preferred_element_type=F32)
    added = added[:, :lanes] + added[:, lanes:]
    chunk_decay = jnp.exp(-rate_lane * float(CHUNK))
    state = jnp.zeros((channels, lanes), F32)
    states = []
    for k in range(count):
        states.append(state)
        chunk = jnp.where(own, added[k * channels:(k + 1) * channels], 0.0)
        state = chunk_decay * state + chunk
    state_out[...] = state

    pl.semaphore_wait(barrier, n_ctx - 1 + n_chan - 1)
    state_copies = []
    for step in range(1, n_ctx):
        copy = pltpu.make_async_remote_copy(
            src_ref=state_out,
            dst_ref=state_in.at[step - 1],
            send_sem=state_send.at[step - 1],
            recv_sem=state_recv.at[step - 1],
            device_id={"ctx": lax.rem(ctx + step, n_ctx)},
            device_id_type=MESH,
        )
        copy.start()
        state_copies.append(copy)

    loads["skip"].wait()
    taps = taps + jnp.where(token == 0, column_of(skip_ref, channels), 0.0)
    target = lax.broadcasted_iota(jnp.int32, (CHUNK, CHUNK), 1)
    source = lax.broadcasted_iota(jnp.int32, (CHUNK, CHUNK), 0)
    channel_of = lax.broadcasted_iota(jnp.int32, (count * channels, CHUNK), 0) % channels
    left, right = [], []
    for c in range(channels):
        wide = jnp.broadcast_to(taps[c:c + 1], (CHUNK, CHUNK))
        turned = pltpu.roll(wide, 0, 1, stride=1, stride_axis=0)
        toeplitz = jnp.where(target >= source, turned, 0.0)
        right.append(jnp.concatenate(two_terms(toeplitz), axis=1))
        left.append(jnp.where(channel_of == c, signal, 0.0).astype(BF16))
    near = jnp.dot(
        jnp.concatenate(left, axis=1), jnp.concatenate(right, axis=0), preferred_element_type=F32
    )
    leave = weight_lane * jnp.exp(-rate_lane * (place + 1.0))
    leave2 = jnp.concatenate(two_terms(leave), axis=0)
    leave2 = jnp.concatenate([leave2, leave2], axis=1)
    power = jnp.exp(
        -rate_lane * (float(CHUNK) * lax.broadcasted_iota(jnp.int32, (count, lanes), 0).astype(F32))
    )

    for name in ("residual", "gate", "gain"):
        loads[name].wait()

    carry = jnp.zeros((channels, lanes), F32)
    for step in range(1, n_ctx):
        state_copies[step - 1].wait()
        decay = jnp.exp(-rate_lane * float(local_len * (step - 1)))
        carry = carry + jnp.where(ctx >= step, decay, 0.0) * state_in[step - 1]
    full = jnp.concatenate([states[k] + power[k:k + 1] * carry for k in range(count)], axis=0)
    far = lax.dot_general(
        jnp.concatenate(two_terms(full), axis=1), leave2, (((1,), (1,)), ((), ())),
        preferred_element_type=F32,
    )
    both = near + far
    conv = both[:, :CHUNK] + both[:, CHUNK:]
    mixed = stack_chunks(residual_ref[...], count) + stack_chunks(gate_ref[...].astype(F32), count) * conv
    square_out[...] = jnp.sum((mixed * mixed).reshape(count, channels, CHUNK), axis=1)

    square_copies = []
    for step in range(1, n_chan):
        copy = pltpu.make_async_remote_copy(
            src_ref=square_out,
            dst_ref=square_in.at[step - 1],
            send_sem=square_send.at[step - 1],
            recv_sem=square_recv.at[step - 1],
            device_id={"chan": lax.rem(chan + step, n_chan)},
            device_id_type=MESH,
        )
        copy.start()
        square_copies.append(copy)
    gain = column_of(gain_ref, channels)
    for k in range(count):
        mixed_ref[:, k * CHUNK:(k + 1) * CHUNK] = mixed[k * channels:(k + 1) * channels]
    total = square_out[...]
    for step in range(1, n_chan):
        square_copies[step - 1].wait()
        total = total + square_in[step - 1]
    scale = lax.rsqrt(total / float(channels * n_chan) + 1e-06)
    for k in range(count):
        normed = mixed[k * channels:(k + 1) * channels] * scale[k:k + 1] * gain
        normed_ref[:, k * CHUNK:(k + 1) * CHUNK] = normed.astype(BF16)


def local(n_ctx, n_chan, value, gate, residual, rates, residues, skip, gain):
    channels, local_len = value.shape
    lanes = channels * rates.shape[1]
    count = local_len // CHUNK
    vmem = pl.BlockSpec(memory_space=pltpu.VMEM)
    hbm = pl.BlockSpec(memory_space=pltpu.HBM)
    return pl.pallas_call(
        functools.partial(kernel, n_ctx, n_chan),
        out_shape=(
            jax.ShapeDtypeStruct((channels, local_len), F32),
            jax.ShapeDtypeStruct((channels, local_len), BF16),
        ),
        in_specs=[hbm] * 7,
        out_specs=(vmem, vmem),
        scratch_shapes=[
            pltpu.VMEM(rates.shape, F32),
            pltpu.VMEM(residues.shape, F32),
            pltpu.VMEM(value.shape, BF16),
            pltpu.SMEM(skip.shape, F32),
            pltpu.VMEM(residual.shape, F32),
            pltpu.VMEM(gate.shape, BF16),
            pltpu.SMEM(gain.shape, F32),
            pltpu.SemaphoreType.DMA((7,)),
            pltpu.VMEM((channels, lanes), F32),
            pltpu.VMEM((n_ctx - 1, channels, lanes), F32),
            pltpu.VMEM((count, CHUNK), F32),
            pltpu.VMEM((n_chan - 1, count, CHUNK), F32),
            pltpu.SemaphoreType.DMA((n_ctx - 1,)),
            pltpu.SemaphoreType.DMA((n_ctx - 1,)),
            pltpu.SemaphoreType.DMA((n_chan - 1,)),
            pltpu.SemaphoreType.DMA((n_chan - 1,)),
        ],
        compiler_params=pltpu.CompilerParams(
            collective_id=0, has_side_effects=True, vmem_limit_bytes=32 * 1024 * 1024
        ),
        cost_estimate=pl.CostEstimate(
            flops=2 * count * channels * CHUNK * 2 * (channels * CHUNK + 3 * lanes),
            bytes_accessed=14 * channels * local_len,
            transcendentals=64 * 1024,
        ),
    )(*[
        pltpu.with_memory_space_constraint(x, pltpu.HBM)
        for x in (value, gate, residual, rates, residues, skip, gain)
    ])


def solution(mesh):
    return jax.shard_map(
        functools.partial(local, mesh.shape["ctx"], mesh.shape["chan"]),
        mesh=mesh,
        in_specs=(
            P("chan", "ctx"),
            P("chan", "ctx"),
            P("chan", "ctx"),
            P("chan", None),
            P("chan", None),
            P("chan"),
            P("chan"),
        ),
        out_specs=(P("chan", "ctx"), P("chan", "ctx")),
        check_vma=False,
    )
```

```python
import functools

import jax
import jax.numpy as jnp
from jax import lax
from jax.experimental import pallas as pl
from jax.experimental.pallas import tpu as pltpu
from jax.sharding import PartitionSpec as P

CHUNK = 128
F32 = jnp.float32
BF16 = jnp.bfloat16
MESH = pl.DeviceIdType.MESH


def two_terms(x):
    high = x.astype(BF16)
    return high, (x - high.astype(F32)).astype(BF16)


def stack_chunks(x, count):
    return jnp.concatenate([x[:, k * CHUNK:(k + 1) * CHUNK] for k in range(count)], axis=0)


def column_of(ref, count):
    row = lax.broadcasted_iota(jnp.int32, (count, CHUNK), 0)
    out = jnp.zeros((count, CHUNK), F32)
    for c in range(count):
        out = jnp.where(row == c, ref[c], out)
    return out


def kernel(
    n_ctx, n_chan,
    value_hbm, gate_hbm, residual_hbm, rates_hbm, residues_hbm, skip_hbm, gain_hbm,
    mixed_ref, normed_ref,
    rates_ref, residues_ref, value_ref, skip_ref, residual_ref, gate_ref, gain_ref, load_sem,
    carry_ref, state_out, state_in, square_out, square_in,
    state_send, state_recv, square_send, square_recv,
):
    loads = {}
    for order, (name, source, target) in enumerate([
        ("rates", rates_hbm, rates_ref),
        ("residues", residues_hbm, residues_ref),
        ("value", value_hbm, value_ref),
        ("skip", skip_hbm, skip_ref),
        ("residual", residual_hbm, residual_ref),
        ("gate", gate_hbm, gate_ref),
        ("gain", gain_hbm, gain_ref),
    ]):
        loads[name] = pltpu.make_async_copy(source, target, load_sem.at[order])
        loads[name].start()
    ctx = lax.axis_index("ctx")
    chan = lax.axis_index("chan")
    channels, local_len = value_ref.shape
    modes = rates_ref.shape[1]
    lanes = channels * modes
    count = local_len // CHUNK

    barrier = pltpu.get_barrier_semaphore()
    for step in range(1, n_ctx):
        @pl.when(ctx >= step)
        def _():
            pl.semaphore_signal(
                barrier, inc=1, device_id={"ctx": lax.rem(ctx - step + n_ctx, n_ctx)}, device_id_type=MESH
            )
    for step in range(1, n_chan):
        pl.semaphore_signal(
            barrier, inc=1, device_id={"chan": lax.rem(chan + step, n_chan)}, device_id_type=MESH
        )

    loads["rates"].wait()
    loads["residues"].wait()
    rates = rates_ref[...]
    weights = residues_ref[...] * jnp.sqrt(2.0 * rates)
    row8 = lax.broadcasted_iota(jnp.int32, (channels, lanes), 0)
    lane8 = lax.broadcasted_iota(jnp.int32, (channels, lanes), 1)
    token = lax.broadcasted_iota(jnp.int32, (channels, CHUNK), 1)
    time = token.astype(F32)
    taps = jnp.zeros((channels, CHUNK), F32)
    rate_rows = jnp.zeros((channels, lanes), F32)
    weight_rows = jnp.zeros((channels, lanes), F32)
    for m in range(modes):
        rate = jnp.broadcast_to(rates[:, m:m + 1], (channels, CHUNK))
        weight = jnp.broadcast_to(weights[:, m:m + 1], (channels, CHUNK))
        taps = taps + weight * jnp.exp(-rate * time)
        here = lane8 % modes == m
        rate_rows = jnp.where(here, rate, rate_rows)
        weight_rows = jnp.where(here, weight, weight_rows)
    own = row8 == lane8 // modes
    rate_lane = jnp.sum(jnp.where(own, rate_rows, 0.0), axis=0, keepdims=True)
    weight_lane = jnp.sum(jnp.where(own, weight_rows, 0.0), axis=0, keepdims=True)

    loads["value"].wait()
    signal = stack_chunks(value_ref[...].astype(F32), count)
    signal16 = signal.astype(BF16)
    place = lax.broadcasted_iota(jnp.int32, (CHUNK, lanes), 0).astype(F32)
    enter = jnp.exp(-rate_lane * (CHUNK - 1.0 - place))
    enter2 = jnp.concatenate(two_terms(enter), axis=1)
    added = jnp.dot(signal16, enter2, preferred_element_type=F32)
    added = added[:, :lanes] + added[:, lanes:]
    chunk_decay = jnp.exp(-rate_lane * float(CHUNK))
    state = jnp.zeros((channels, lanes), F32)
    states = []
    for k in range(count):
        states.append(state)
        chunk = jnp.where(own, added[k * channels:(k + 1) * channels], 0.0)
        state = chunk_decay * state + chunk
    state_out[...] = state

    pl.semaphore_wait(barrier, n_ctx - 1 - ctx + n_chan - 1)
    state_copies = []
    for step in range(1, n_ctx):
        copy = pltpu.make_async_remote_copy(
            src_ref=state_out,
            dst_ref=state_in.at[step - 1],
            send_sem=state_send.at[step - 1],
            recv_sem=state_recv.at[step - 1],
            device_id={"ctx": lax.rem(ctx + step, n_ctx)},
            device_id_type=MESH,
        )
        pl.when(ctx + step < n_ctx)(copy.start)
        state_copies.append(copy)

    loads["skip"].wait()
    taps = taps + jnp.where(token == 0, column_of(skip_ref, channels), 0.0)
    target = lax.broadcasted_iota(jnp.int32, (CHUNK, CHUNK), 1)
    source = lax.broadcasted_iota(jnp.int32, (CHUNK, CHUNK), 0)
    channel_of = lax.broadcasted_iota(jnp.int32, (count * channels, CHUNK), 0) % channels
    left, right = [], []
    for c in range(channels):
        wide = jnp.broadcast_to(taps[c:c + 1], (CHUNK, CHUNK))
        turned = pltpu.roll(wide, 0, 1, stride=1, stride_axis=0)
        toeplitz = jnp.where(target >= source, turned, 0.0)
        right.append(jnp.concatenate(two_terms(toeplitz), axis=1))
        left.append(jnp.where(channel_of == c, signal, 0.0).astype(BF16))
    near = jnp.dot(
        jnp.concatenate(left, axis=1), jnp.concatenate(right, axis=0), preferred_element_type=F32
    )
    leave = weight_lane * jnp.exp(-rate_lane * (place + 1.0))
    leave2 = jnp.concatenate(two_terms(leave), axis=0)
    leave2 = jnp.concatenate([leave2, leave2], axis=1)
    power = jnp.exp(
        -rate_lane * (float(CHUNK) * lax.broadcasted_iota(jnp.int32, (count, lanes), 0).astype(F32))
    )

    for name in ("residual", "gate", "gain"):
        loads[name].wait()

    carry_ref[...] = jnp.zeros((channels, lanes), F32)
    for step in range(1, n_ctx):
        decay = jnp.exp(-rate_lane * float(local_len * (step - 1)))

        @pl.when(ctx >= step)
        def _():
            state_copies[step - 1].wait_recv()
            carry_ref[...] += decay * state_in[step - 1]
    carry = carry_ref[...]
    full = jnp.concatenate([states[k] + power[k:k + 1] * carry for k in range(count)], axis=0)
    far = lax.dot_general(
        jnp.concatenate(two_terms(full), axis=1), leave2, (((1,), (1,)), ((), ())),
        preferred_element_type=F32,
    )
    both = near + far
    conv = both[:, :CHUNK] + both[:, CHUNK:]
    mixed = stack_chunks(residual_ref[...], count) + stack_chunks(gate_ref[...].astype(F32), count) * conv
    square_out[...] = jnp.sum((mixed * mixed).reshape(count, channels, CHUNK), axis=1)

    square_copies = []
    for step in range(1, n_chan):
        copy = pltpu.make_async_remote_copy(
            src_ref=square_out,
            dst_ref=square_in.at[step - 1],
            send_sem=square_send.at[step - 1],
            recv_sem=square_recv.at[step - 1],
            device_id={"chan": lax.rem(chan + step, n_chan)},
            device_id_type=MESH,
        )
        copy.start()
        square_copies.append(copy)
    gain = column_of(gain_ref, channels)
    for k in range(count):
        mixed_ref[:, k * CHUNK:(k + 1) * CHUNK] = mixed[k * channels:(k + 1) * channels]
    total = square_out[...]
    for step in range(1, n_chan):
        square_copies[step - 1].wait()
        total = total + square_in[step - 1]
    for step in range(1, n_ctx):
        pl.when(ctx + step < n_ctx)(state_copies[step - 1].wait_send)
    scale = lax.rsqrt(total / float(channels * n_chan) + 1e-06)
    for k in range(count):
        normed = mixed[k * channels:(k + 1) * channels] * scale[k:k + 1] * gain
        normed_ref[:, k * CHUNK:(k + 1) * CHUNK] = normed.astype(BF16)


def local(n_ctx, n_chan, value, gate, residual, rates, residues, skip, gain):
    channels, local_len = value.shape
    lanes = channels * rates.shape[1]
    count = local_len // CHUNK
    vmem = pl.BlockSpec(memory_space=pltpu.VMEM)
    hbm = pl.BlockSpec(memory_space=pltpu.HBM)
    return pl.pallas_call(
        functools.partial(kernel, n_ctx, n_chan),
        out_shape=(
            jax.ShapeDtypeStruct((channels, local_len), F32),
            jax.ShapeDtypeStruct((channels, local_len), BF16),
        ),
        in_specs=[hbm] * 7,
        out_specs=(vmem, vmem),
        scratch_shapes=[
            pltpu.VMEM(rates.shape, F32),
            pltpu.VMEM(residues.shape, F32),
            pltpu.VMEM(value.shape, BF16),
            pltpu.SMEM(skip.shape, F32),
            pltpu.VMEM(residual.shape, F32),
            pltpu.VMEM(gate.shape, BF16),
            pltpu.SMEM(gain.shape, F32),
            pltpu.SemaphoreType.DMA((7,)),
            pltpu.VMEM((channels, lanes), F32),
            pltpu.VMEM((channels, lanes), F32),
            pltpu.VMEM((n_ctx - 1, channels, lanes), F32),
            pltpu.VMEM((count, CHUNK), F32),
            pltpu.VMEM((n_chan - 1, count, CHUNK), F32),
            pltpu.SemaphoreType.DMA((n_ctx - 1,)),
            pltpu.SemaphoreType.DMA((n_ctx - 1,)),
            pltpu.SemaphoreType.DMA((n_chan - 1,)),
            pltpu.SemaphoreType.DMA((n_chan - 1,)),
        ],
        compiler_params=pltpu.CompilerParams(
            collective_id=0, has_side_effects=True, vmem_limit_bytes=32 * 1024 * 1024
        ),
        cost_estimate=pl.CostEstimate(
            flops=2 * count * channels * CHUNK * 2 * (channels * CHUNK + 3 * lanes),
            bytes_accessed=14 * channels * local_len,
            transcendentals=64 * 1024,
        ),
    )(*[
        pltpu.with_memory_space_constraint(x, pltpu.HBM)
        for x in (value, gate, residual, rates, residues, skip, gain)
    ])


def solution(mesh):
    return jax.shard_map(
        functools.partial(local, mesh.shape["ctx"], mesh.shape["chan"]),
        mesh=mesh,
        in_specs=(
            P("chan", "ctx"),
            P("chan", "ctx"),
            P("chan", "ctx"),
            P("chan", None),
            P("chan", None),
            P("chan"),
            P("chan"),
        ),
        out_specs=(P("chan", "ctx"), P("chan", "ctx")),
        check_vma=False,
    )
```

```python
import functools

import jax
import jax.numpy as jnp
from jax import lax
from jax.experimental import pallas as pl
from jax.experimental.pallas import tpu as pltpu
from jax.sharding import PartitionSpec as P

CHUNK = 128
F32 = jnp.float32
BF16 = jnp.bfloat16
MESH = pl.DeviceIdType.MESH


def two_terms(x):
    high = x.astype(BF16)
    return high, (x - high.astype(F32)).astype(BF16)


def stack_chunks(x, count):
    return jnp.concatenate([x[:, k * CHUNK:(k + 1) * CHUNK] for k in range(count)], axis=0)


def column_of(ref, count):
    row = lax.broadcasted_iota(jnp.int32, (count, CHUNK), 0)
    out = jnp.zeros((count, CHUNK), F32)
    for c in range(count):
        out = jnp.where(row == c, ref[c], out)
    return out


def kernel(
    n_ctx, n_chan,
    value_hbm, gate_hbm, residual_hbm, rates_hbm, residues_hbm, skip_hbm, gain_hbm,
    mixed_ref, normed_ref,
    rates_ref, residues_ref, value_ref, skip_ref, residual_ref, gate_ref, gain_ref, load_sem,
    carry_ref, state_out, state_in, square_out, square_in,
    state_send, state_recv, square_send, square_recv,
):
    loads = {}
    for order, (name, source, target) in enumerate([
        ("rates", rates_hbm, rates_ref),
        ("residues", residues_hbm, residues_ref),
        ("value", value_hbm, value_ref),
        ("skip", skip_hbm, skip_ref),
        ("residual", residual_hbm, residual_ref),
        ("gate", gate_hbm, gate_ref),
        ("gain", gain_hbm, gain_ref),
    ]):
        loads[name] = pltpu.make_async_copy(source, target, load_sem.at[order])
        loads[name].start()
    ctx = lax.axis_index("ctx")
    chan = lax.axis_index("chan")
    channels, local_len = value_ref.shape
    modes = rates_ref.shape[1]
    lanes = channels * modes
    count = local_len // CHUNK

    barrier = pltpu.get_barrier_semaphore()
    for step in range(1, n_ctx):
        @pl.when(ctx >= step)
        def _():
            pl.semaphore_signal(
                barrier, inc=1, device_id={"ctx": lax.rem(ctx - step + n_ctx, n_ctx)}, device_id_type=MESH
            )
    for step in range(1, n_chan):
        pl.semaphore_signal(
            barrier, inc=1, device_id={"chan": lax.rem(chan + step, n_chan)}, device_id_type=MESH
        )

    loads["rates"].wait()
    loads["residues"].wait()
    rates = rates_ref[...]
    weights = residues_ref[...] * jnp.sqrt(2.0 * rates)
    row8 = lax.broadcasted_iota(jnp.int32, (channels, lanes), 0)
    lane8 = lax.broadcasted_iota(jnp.int32, (channels, lanes), 1)
    token = lax.broadcasted_iota(jnp.int32, (channels, CHUNK), 1)
    time = token.astype(F32)
    taps = jnp.zeros((channels, CHUNK), F32)
    rate_rows = jnp.zeros((channels, lanes), F32)
    weight_rows = jnp.zeros((channels, lanes), F32)
    for m in range(modes):
        rate = jnp.broadcast_to(rates[:, m:m + 1], (channels, CHUNK))
        weight = jnp.broadcast_to(weights[:, m:m + 1], (channels, CHUNK))
        taps = taps + weight * jnp.exp(-rate * time)
        here = lane8 % modes == m
        rate_rows = jnp.where(here, rate, rate_rows)
        weight_rows = jnp.where(here, weight, weight_rows)
    own = row8 == lane8 // modes
    rate_lane = jnp.sum(jnp.where(own, rate_rows, 0.0), axis=0, keepdims=True)
    weight_lane = jnp.sum(jnp.where(own, weight_rows, 0.0), axis=0, keepdims=True)

    loads["value"].wait()
    signal = stack_chunks(value_ref[...].astype(F32), count)
    signal16 = signal.astype(BF16)
    place = lax.broadcasted_iota(jnp.int32, (CHUNK, lanes), 0).astype(F32)
    enter = jnp.exp(-rate_lane * (CHUNK - 1.0 - place))
    enter2 = jnp.concatenate(two_terms(enter), axis=1)
    added = jnp.dot(signal16, enter2, preferred_element_type=F32)
    added = added[:, :lanes] + added[:, lanes:]
    chunk_decay = jnp.exp(-rate_lane * float(CHUNK))
    state = jnp.zeros((channels, lanes), F32)
    states = []
    for k in range(count):
        states.append(state)
        chunk = jnp.where(own, added[k * channels:(k + 1) * channels], 0.0)
        state = chunk_decay * state + chunk
    state_out[...] = state

    pl.semaphore_wait(barrier, n_ctx - 1 - ctx + n_chan - 1)
    state_copies = []
    for step in range(1, n_ctx):
        copy = pltpu.make_async_remote_copy(
            src_ref=state_out,
            dst_ref=state_in.at[step - 1],
            send_sem=state_send.at[step - 1],
            recv_sem=state_recv.at[step - 1],
            device_id={"ctx": lax.rem(ctx + step, n_ctx)},
            device_id_type=MESH,
        )
        pl.when(ctx + step < n_ctx)(copy.start)
        state_copies.append(copy)

    loads["skip"].wait()
    taps = taps + jnp.where(token == 0, column_of(skip_ref, channels), 0.0)
    target = lax.broadcasted_iota(jnp.int32, (CHUNK, CHUNK), 1)
    source = lax.broadcasted_iota(jnp.int32, (CHUNK, CHUNK), 0)
    channel_of = lax.broadcasted_iota(jnp.int32, (count * channels, CHUNK), 0) % channels
    left, right = [], []
    for c in range(channels):
        wide = jnp.broadcast_to(taps[c:c + 1], (CHUNK, CHUNK))
        turned = pltpu.roll(wide, 0, 1, stride=1, stride_axis=0)
        toeplitz = jnp.where(target >= source, turned, 0.0)
        right.append(jnp.concatenate(two_terms(toeplitz), axis=1))
        left.append(jnp.where(channel_of == c, signal, 0.0).astype(BF16))
    close = jnp.dot(
        jnp.concatenate(left, axis=1), jnp.concatenate(right, axis=0), preferred_element_type=F32
    )
    leave = weight_lane * jnp.exp(-rate_lane * (place + 1.0))
    leave2 = jnp.concatenate(two_terms(leave), axis=0)
    leave2 = jnp.concatenate([leave2, leave2], axis=1)
    inside = lax.dot_general(
        jnp.concatenate(two_terms(jnp.concatenate(states, axis=0)), axis=1), leave2,
        (((1,), (1,)), ((), ())), preferred_element_type=F32,
    )
    near = close + inside
    near = near[:, :CHUNK] + near[:, CHUNK:]
    power = jnp.exp(
        -rate_lane * (float(CHUNK) * lax.broadcasted_iota(jnp.int32, (count, lanes), 0).astype(F32))
    )
    power = jnp.concatenate([jnp.where(own, power[k:k + 1], 0.0) for k in range(count)], axis=0)
    power2 = jnp.concatenate(two_terms(power), axis=1)
    for name in ("residual", "gate", "gain"):
        loads[name].wait()
    gate = stack_chunks(gate_ref[...].astype(F32), count)
    base = stack_chunks(residual_ref[...], count) + gate * near
    gain = column_of(gain_ref, channels)

    carry_ref[...] = jnp.zeros((channels, lanes), F32)
    for step in range(1, n_ctx):
        decay = jnp.exp(-rate_lane * float(local_len * (step - 1)))

        @pl.when(ctx >= step)
        def _():
            state_copies[step - 1].wait_recv()
            carry_ref[...] += decay * state_in[step - 1]
    carry = jnp.sum(carry_ref[...], axis=0, keepdims=True)
    arrive2 = jnp.concatenate(two_terms(leave * carry), axis=0)
    far = lax.dot_general(
        power2, jnp.concatenate([arrive2, arrive2], axis=1), (((1,), (1,)), ((), ())),
        preferred_element_type=F32,
    )
    mixed = base + gate * (far[:, :CHUNK] + far[:, CHUNK:])
    square_out[...] = jnp.sum((mixed * mixed).reshape(count, channels, CHUNK), axis=1)

    square_copies = []
    for step in range(1, n_chan):
        copy = pltpu.make_async_remote_copy(
            src_ref=square_out,
            dst_ref=square_in.at[step - 1],
            send_sem=square_send.at[step - 1],
            recv_sem=square_recv.at[step - 1],
            device_id={"chan": lax.rem(chan + step, n_chan)},
            device_id_type=MESH,
        )
        copy.start()
        square_copies.append(copy)
    gained = []
    for k in range(count):
        chunk = mixed[k * channels:(k + 1) * channels]
        mixed_ref[:, k * CHUNK:(k + 1) * CHUNK] = chunk
        gained.append(chunk * gain)
    for step in range(1, n_ctx):
        pl.when(ctx + step < n_ctx)(state_copies[step - 1].wait_send)
    total = square_out[...]
    for step in range(1, n_chan):
        square_copies[step - 1].wait_recv()
        total = total + square_in[step - 1]
    scale = lax.rsqrt(total / float(channels * n_chan) + 1e-06)
    for k in range(count):
        normed_ref[:, k * CHUNK:(k + 1) * CHUNK] = (gained[k] * scale[k:k + 1]).astype(BF16)
    for step in range(1, n_chan):
        square_copies[step - 1].wait_send()


def local(n_ctx, n_chan, value, gate, residual, rates, residues, skip, gain):
    channels, local_len = value.shape
    lanes = channels * rates.shape[1]
    count = local_len // CHUNK
    vmem = pl.BlockSpec(memory_space=pltpu.VMEM)
    hbm = pl.BlockSpec(memory_space=pltpu.HBM)
    return pl.pallas_call(
        functools.partial(kernel, n_ctx, n_chan),
        out_shape=(
            jax.ShapeDtypeStruct((channels, local_len), F32),
            jax.ShapeDtypeStruct((channels, local_len), BF16),
        ),
        in_specs=[hbm] * 7,
        out_specs=(vmem, vmem),
        scratch_shapes=[
            pltpu.VMEM(rates.shape, F32),
            pltpu.VMEM(residues.shape, F32),
            pltpu.VMEM(value.shape, BF16),
            pltpu.SMEM(skip.shape, F32),
            pltpu.VMEM(residual.shape, F32),
            pltpu.VMEM(gate.shape, BF16),
            pltpu.SMEM(gain.shape, F32),
            pltpu.SemaphoreType.DMA((7,)),
            pltpu.VMEM((channels, lanes), F32),
            pltpu.VMEM((channels, lanes), F32),
            pltpu.VMEM((n_ctx - 1, channels, lanes), F32),
            pltpu.VMEM((count, CHUNK), F32),
            pltpu.VMEM((n_chan - 1, count, CHUNK), F32),
            pltpu.SemaphoreType.DMA((n_ctx - 1,)),
            pltpu.SemaphoreType.DMA((n_ctx - 1,)),
            pltpu.SemaphoreType.DMA((n_chan - 1,)),
            pltpu.SemaphoreType.DMA((n_chan - 1,)),
        ],
        compiler_params=pltpu.CompilerParams(
            collective_id=0, has_side_effects=True, vmem_limit_bytes=32 * 1024 * 1024
        ),
        cost_estimate=pl.CostEstimate(
            flops=2 * count * channels * CHUNK * 2 * (channels * CHUNK + 3 * lanes),
            bytes_accessed=14 * channels * local_len,
            transcendentals=64 * 1024,
        ),
    )(*[
        pltpu.with_memory_space_constraint(x, pltpu.HBM)
        for x in (value, gate, residual, rates, residues, skip, gain)
    ])


def solution(mesh):
    return jax.shard_map(
        functools.partial(local, mesh.shape["ctx"], mesh.shape["chan"]),
        mesh=mesh,
        in_specs=(
            P("chan", "ctx"),
            P("chan", "ctx"),
            P("chan", "ctx"),
            P("chan", None),
            P("chan", None),
            P("chan"),
            P("chan"),
        ),
        out_specs=(P("chan", "ctx"), P("chan", "ctx")),
        check_vma=False,
    )
```

```python
import functools

import jax
import jax.numpy as jnp
from jax import lax
from jax.experimental import pallas as pl
from jax.experimental.pallas import tpu as pltpu
from jax.sharding import PartitionSpec as P

CHUNK = 128
F32 = jnp.float32
BF16 = jnp.bfloat16
MESH = pl.DeviceIdType.MESH


def two_terms(x):
    high = x.astype(BF16)
    return high, (x - high.astype(F32)).astype(BF16)


def stack_chunks(x, count):
    return jnp.concatenate([x[:, k * CHUNK:(k + 1) * CHUNK] for k in range(count)], axis=0)


def column_of(ref, count):
    row = lax.broadcasted_iota(jnp.int32, (count, CHUNK), 0)
    out = jnp.zeros((count, CHUNK), F32)
    for c in range(count):
        out = jnp.where(row == c, ref[c], out)
    return out


def kernel(
    n_ctx, n_chan,
    value_hbm, gate_hbm, residual_hbm, rates_hbm, residues_hbm, skip_hbm, gain_hbm,
    base_out, added_out, scale_out,
    rates_ref, residues_ref, value_ref, skip_ref, residual_ref, gate_ref, gain_ref, load_sem,
    carry_ref, state_out, state_in, square_out, square_in,
    state_send, state_recv, square_send, square_recv,
):
    loads = {}
    for order, (name, source, target) in enumerate([
        ("rates", rates_hbm, rates_ref),
        ("residues", residues_hbm, residues_ref),
        ("value", value_hbm, value_ref),
        ("skip", skip_hbm, skip_ref),
        ("residual", residual_hbm, residual_ref),
        ("gate", gate_hbm, gate_ref),
        ("gain", gain_hbm, gain_ref),
    ]):
        loads[name] = pltpu.make_async_copy(source, target, load_sem.at[order])
        loads[name].start()
    ctx = lax.axis_index("ctx")
    chan = lax.axis_index("chan")
    channels, local_len = value_ref.shape
    modes = rates_ref.shape[1]
    lanes = channels * modes
    count = local_len // CHUNK

    barrier = pltpu.get_barrier_semaphore()
    for step in range(1, n_ctx):
        @pl.when(ctx >= step)
        def _():
            pl.semaphore_signal(
                barrier, inc=1, device_id={"ctx": lax.rem(ctx - step + n_ctx, n_ctx)}, device_id_type=MESH
            )
    for step in range(1, n_chan):
        pl.semaphore_signal(
            barrier, inc=1, device_id={"chan": lax.rem(chan + step, n_chan)}, device_id_type=MESH
        )

    loads["rates"].wait()
    loads["residues"].wait()
    rates = rates_ref[...]
    weights = residues_ref[...] * jnp.sqrt(2.0 * rates)
    row8 = lax.broadcasted_iota(jnp.int32, (channels, lanes), 0)
    lane8 = lax.broadcasted_iota(jnp.int32, (channels, lanes), 1)
    token = lax.broadcasted_iota(jnp.int32, (channels, CHUNK), 1)
    time = token.astype(F32)
    taps = jnp.zeros((channels, CHUNK), F32)
    rate_rows = jnp.zeros((channels, lanes), F32)
    weight_rows = jnp.zeros((channels, lanes), F32)
    for m in range(modes):
        rate = jnp.broadcast_to(rates[:, m:m + 1], (channels, CHUNK))
        weight = jnp.broadcast_to(weights[:, m:m + 1], (channels, CHUNK))
        taps = taps + weight * jnp.exp(-rate * time)
        here = lane8 % modes == m
        rate_rows = jnp.where(here, rate, rate_rows)
        weight_rows = jnp.where(here, weight, weight_rows)
    own = row8 == lane8 // modes
    rate_lane = jnp.sum(jnp.where(own, rate_rows, 0.0), axis=0, keepdims=True)
    weight_lane = jnp.sum(jnp.where(own, weight_rows, 0.0), axis=0, keepdims=True)

    loads["value"].wait()
    signal = stack_chunks(value_ref[...].astype(F32), count)
    signal16 = signal.astype(BF16)
    place = lax.broadcasted_iota(jnp.int32, (CHUNK, lanes), 0).astype(F32)
    enter = jnp.exp(-rate_lane * (CHUNK - 1.0 - place))
    enter2 = jnp.concatenate(two_terms(enter), axis=1)
    added = jnp.dot(signal16, enter2, preferred_element_type=F32)
    added = added[:, :lanes] + added[:, lanes:]
    chunk_decay = jnp.exp(-rate_lane * float(CHUNK))
    state = jnp.zeros((channels, lanes), F32)
    states = []
    for k in range(count):
        states.append(state)
        chunk = jnp.where(own, added[k * channels:(k + 1) * channels], 0.0)
        state = chunk_decay * state + chunk
    state_out[...] = state

    pl.semaphore_wait(barrier, n_ctx - 1 - ctx + n_chan - 1)
    state_copies = []
    for step in range(1, n_ctx):
        copy = pltpu.make_async_remote_copy(
            src_ref=state_out,
            dst_ref=state_in.at[step - 1],
            send_sem=state_send.at[step - 1],
            recv_sem=state_recv.at[step - 1],
            device_id={"ctx": lax.rem(ctx + step, n_ctx)},
            device_id_type=MESH,
        )
        pl.when(ctx + step < n_ctx)(copy.start)
        state_copies.append(copy)

    loads["skip"].wait()
    taps = taps + jnp.where(token == 0, column_of(skip_ref, channels), 0.0)
    target = lax.broadcasted_iota(jnp.int32, (CHUNK, CHUNK), 1)
    source = lax.broadcasted_iota(jnp.int32, (CHUNK, CHUNK), 0)
    channel_of = lax.broadcasted_iota(jnp.int32, (count * channels, CHUNK), 0) % channels
    left, right = [], []
    for c in range(channels):
        wide = jnp.broadcast_to(taps[c:c + 1], (CHUNK, CHUNK))
        turned = pltpu.roll(wide, 0, 1, stride=1, stride_axis=0)
        toeplitz = jnp.where(target >= source, turned, 0.0)
        right.append(jnp.concatenate(two_terms(toeplitz), axis=1))
        left.append(jnp.where(channel_of == c, signal, 0.0).astype(BF16))
    close = jnp.dot(
        jnp.concatenate(left, axis=1), jnp.concatenate(right, axis=0), preferred_element_type=F32
    )
    leave = weight_lane * jnp.exp(-rate_lane * (place + 1.0))
    leave2 = jnp.concatenate(two_terms(leave), axis=0)
    leave2 = jnp.concatenate([leave2, leave2], axis=1)
    inside = lax.dot_general(
        jnp.concatenate(two_terms(jnp.concatenate(states, axis=0)), axis=1), leave2,
        (((1,), (1,)), ((), ())), preferred_element_type=F32,
    )
    near = close + inside
    near = near[:, :CHUNK] + near[:, CHUNK:]
    power = jnp.exp(
        -rate_lane * (float(CHUNK) * lax.broadcasted_iota(jnp.int32, (count, lanes), 0).astype(F32))
    )
    power = jnp.concatenate([jnp.where(own, power[k:k + 1], 0.0) for k in range(count)], axis=0)
    power2 = jnp.concatenate(two_terms(power), axis=1)
    for name in ("residual", "gate", "gain"):
        loads[name].wait()
    gate = stack_chunks(gate_ref[...].astype(F32), count)
    base = stack_chunks(residual_ref[...], count) + gate * near
    gain = column_of(gain_ref, channels)

    carry_ref[...] = jnp.zeros((channels, lanes), F32)
    for step in range(1, n_ctx):
        decay = jnp.exp(-rate_lane * float(local_len * (step - 1)))

        @pl.when(ctx >= step)
        def _():
            state_copies[step - 1].wait_recv()
            carry_ref[...] += decay * state_in[step - 1]
    carry = jnp.sum(carry_ref[...], axis=0, keepdims=True)
    arrive2 = jnp.concatenate(two_terms(leave * carry), axis=0)
    far = lax.dot_general(
        power2, jnp.concatenate([arrive2, arrive2], axis=1), (((1,), (1,)), ((), ())),
        preferred_element_type=F32,
    )
    added = gate * (far[:, :CHUNK] + far[:, CHUNK:])
    mixed = base + added
    square_out[...] = jnp.sum((mixed * mixed).reshape(count, channels, CHUNK), axis=1)

    square_copies = []
    for step in range(1, n_chan):
        copy = pltpu.make_async_remote_copy(
            src_ref=square_out,
            dst_ref=square_in.at[step - 1],
            send_sem=square_send.at[step - 1],
            recv_sem=square_recv.at[step - 1],
            device_id={"chan": lax.rem(chan + step, n_chan)},
            device_id_type=MESH,
        )
        copy.start()
        square_copies.append(copy)
    for k in range(count):
        tokens = slice(k * CHUNK, (k + 1) * CHUNK)
        base_out[:, tokens] = base[k * channels:(k + 1) * channels]
        added_out[:, tokens] = added[k * channels:(k + 1) * channels]
    for step in range(1, n_ctx):
        pl.when(ctx + step < n_ctx)(state_copies[step - 1].wait_send)
    total = square_out[...]
    for step in range(1, n_chan):
        square_copies[step - 1].wait_recv()
        total = total + square_in[step - 1]
    scale = lax.rsqrt(total / float(channels * n_chan) + 1e-06)
    for k in range(count):
        scale_out[:, k * CHUNK:(k + 1) * CHUNK] = gain * scale[k:k + 1]
    for step in range(1, n_chan):
        square_copies[step - 1].wait_send()


def local(n_ctx, n_chan, value, gate, residual, rates, residues, skip, gain):
    channels, local_len = value.shape
    lanes = channels * rates.shape[1]
    count = local_len // CHUNK
    vmem = pl.BlockSpec(memory_space=pltpu.VMEM)
    hbm = pl.BlockSpec(memory_space=pltpu.HBM)
    base, added, scale = pl.pallas_call(
        functools.partial(kernel, n_ctx, n_chan),
        out_shape=(
            jax.ShapeDtypeStruct((channels, local_len), F32),
            jax.ShapeDtypeStruct((channels, local_len), F32),
            jax.ShapeDtypeStruct((channels, local_len), F32),
        ),
        in_specs=[hbm] * 7,
        out_specs=(vmem, vmem, vmem),
        scratch_shapes=[
            pltpu.VMEM(rates.shape, F32),
            pltpu.VMEM(residues.shape, F32),
            pltpu.VMEM(value.shape, BF16),
            pltpu.SMEM(skip.shape, F32),
            pltpu.VMEM(residual.shape, F32),
            pltpu.VMEM(gate.shape, BF16),
            pltpu.SMEM(gain.shape, F32),
            pltpu.SemaphoreType.DMA((7,)),
            pltpu.VMEM((channels, lanes), F32),
            pltpu.VMEM((channels, lanes), F32),
            pltpu.VMEM((n_ctx - 1, channels, lanes), F32),
            pltpu.VMEM((count, CHUNK), F32),
            pltpu.VMEM((n_chan - 1, count, CHUNK), F32),
            pltpu.SemaphoreType.DMA((n_ctx - 1,)),
            pltpu.SemaphoreType.DMA((n_ctx - 1,)),
            pltpu.SemaphoreType.DMA((n_chan - 1,)),
            pltpu.SemaphoreType.DMA((n_chan - 1,)),
        ],
        compiler_params=pltpu.CompilerParams(
            collective_id=0, has_side_effects=True, vmem_limit_bytes=32 * 1024 * 1024
        ),
        cost_estimate=pl.CostEstimate(
            flops=2 * count * channels * CHUNK * 2 * (channels * CHUNK + 3 * lanes),
            bytes_accessed=14 * channels * local_len,
            transcendentals=64 * 1024,
        ),
    )(*[
        pltpu.with_memory_space_constraint(x, pltpu.HBM)
        for x in (value, gate, residual, rates, residues, skip, gain)
    ])
    mixed = base + added
    return mixed, (mixed * scale).astype(BF16)


def solution(mesh):
    return jax.shard_map(
        functools.partial(local, mesh.shape["ctx"], mesh.shape["chan"]),
        mesh=mesh,
        in_specs=(
            P("chan", "ctx"),
            P("chan", "ctx"),
            P("chan", "ctx"),
            P("chan", None),
            P("chan", None),
            P("chan"),
            P("chan"),
        ),
        out_specs=(P("chan", "ctx"), P("chan", "ctx")),
        check_vma=False,
    )
```

```python
import functools

import jax
import jax.numpy as jnp
from jax import lax
from jax.experimental import pallas as pl
from jax.experimental.pallas import tpu as pltpu
from jax.sharding import PartitionSpec as P

CHUNK = 128
F32 = jnp.float32
BF16 = jnp.bfloat16
MESH = pl.DeviceIdType.MESH


def two_terms(x):
    high = x.astype(BF16)
    return high, (x - high.astype(F32)).astype(BF16)


def stack_chunks(x, count):
    return jnp.concatenate([x[:, k * CHUNK:(k + 1) * CHUNK] for k in range(count)], axis=0)


def column_of(ref, count):
    row = lax.broadcasted_iota(jnp.int32, (count, CHUNK), 0)
    out = jnp.zeros((count, CHUNK), F32)
    for c in range(count):
        out = jnp.where(row == c, ref[c], out)
    return out


def kernel(
    n_ctx, n_chan,
    value_hbm, gate_hbm, residual_hbm, rates_hbm, residues_hbm, skip_hbm, gain_hbm,
    base_out, added_out, scale_out,
    rates_ref, residues_ref, value_ref, skip_ref, residual_ref, gate_ref, gain_ref, load_sem,
    carry_ref, state_out, state_in, square_out, square_in,
    state_send, state_recv, square_send, square_recv,
):
    ctx = lax.axis_index("ctx")
    chan = lax.axis_index("chan")
    channels, local_len = value_ref.shape
    modes = rates_ref.shape[1]
    lanes = channels * modes
    count = local_len // CHUNK

    barrier = pltpu.get_barrier_semaphore()
    for step in range(n_ctx - 1, 0, -1):
        @pl.when(ctx >= step)
        def _():
            pl.semaphore_signal(
                barrier, inc=1, device_id={"ctx": lax.rem(ctx - step + n_ctx, n_ctx)}, device_id_type=MESH
            )
    for step in range(1, n_chan):
        pl.semaphore_signal(
            barrier, inc=1, device_id={"chan": lax.rem(chan + step, n_chan)}, device_id_type=MESH
        )

    loads = {}
    for order, (name, source, target) in enumerate([
        ("rates", rates_hbm, rates_ref),
        ("residues", residues_hbm, residues_ref),
        ("value", value_hbm, value_ref),
        ("skip", skip_hbm, skip_ref),
        ("residual", residual_hbm, residual_ref),
        ("gate", gate_hbm, gate_ref),
        ("gain", gain_hbm, gain_ref),
    ]):
        loads[name] = pltpu.make_async_copy(source, target, load_sem.at[order])
        loads[name].start()

    loads["rates"].wait()
    loads["residues"].wait()
    rates = rates_ref[...]
    weights = residues_ref[...] * jnp.sqrt(2.0 * rates)
    row8 = lax.broadcasted_iota(jnp.int32, (channels, lanes), 0)
    lane8 = lax.broadcasted_iota(jnp.int32, (channels, lanes), 1)
    token = lax.broadcasted_iota(jnp.int32, (channels, CHUNK), 1)
    time = token.astype(F32)
    taps = jnp.zeros((channels, CHUNK), F32)
    rate_rows = jnp.zeros((channels, lanes), F32)
    weight_rows = jnp.zeros((channels, lanes), F32)
    for m in range(modes):
        rate = jnp.broadcast_to(rates[:, m:m + 1], (channels, CHUNK))
        weight = jnp.broadcast_to(weights[:, m:m + 1], (channels, CHUNK))
        taps = taps + weight * jnp.exp(-rate * time)
        here = lane8 % modes == m
        rate_rows = jnp.where(here, rate, rate_rows)
        weight_rows = jnp.where(here, weight, weight_rows)
    own = row8 == lane8 // modes
    rate_lane = jnp.sum(jnp.where(own, rate_rows, 0.0), axis=0, keepdims=True)
    weight_lane = jnp.sum(jnp.where(own, weight_rows, 0.0), axis=0, keepdims=True)

    loads["value"].wait()
    signal = stack_chunks(value_ref[...].astype(F32), count)
    signal16 = signal.astype(BF16)
    place = lax.broadcasted_iota(jnp.int32, (CHUNK, lanes), 0).astype(F32)
    enter = jnp.exp(-rate_lane * (CHUNK - 1.0 - place))
    enter2 = jnp.concatenate(two_terms(enter), axis=1)
    added = jnp.dot(signal16, enter2, preferred_element_type=F32)
    added = added[:, :lanes] + added[:, lanes:]
    chunk_decay = jnp.exp(-rate_lane * float(CHUNK))
    state = jnp.zeros((channels, lanes), F32)
    states = []
    for k in range(count):
        states.append(state)
        chunk = jnp.where(own, added[k * channels:(k + 1) * channels], 0.0)
        state = chunk_decay * state + chunk
    state_out[...] = jnp.sum(state, axis=0, keepdims=True)

    loads["skip"].wait()
    taps = taps + jnp.where(token == 0, column_of(skip_ref, channels), 0.0)
    target = lax.broadcasted_iota(jnp.int32, (CHUNK, CHUNK), 1)
    source = lax.broadcasted_iota(jnp.int32, (CHUNK, CHUNK), 0)
    channel_of = lax.broadcasted_iota(jnp.int32, (count * channels, CHUNK), 0) % channels
    left, right = [], []
    for c in range(channels):
        wide = jnp.broadcast_to(taps[c:c + 1], (CHUNK, CHUNK))
        turned = pltpu.roll(wide, 0, 1, stride=1, stride_axis=0)
        toeplitz = jnp.where(target >= source, turned, 0.0)
        right.append(jnp.concatenate(two_terms(toeplitz), axis=1))
        left.append(jnp.where(channel_of == c, signal, 0.0).astype(BF16))
    close = jnp.dot(
        jnp.concatenate(left, axis=1), jnp.concatenate(right, axis=0), preferred_element_type=F32
    )
    leave = weight_lane * jnp.exp(-rate_lane * (place + 1.0))
    leave2 = jnp.concatenate(two_terms(leave), axis=0)
    leave2 = jnp.concatenate([leave2, leave2], axis=1)
    inside = lax.dot_general(
        jnp.concatenate(two_terms(jnp.concatenate(states, axis=0)), axis=1), leave2,
        (((1,), (1,)), ((), ())), preferred_element_type=F32,
    )
    near = close + inside
    near = near[:, :CHUNK] + near[:, CHUNK:]
    power = jnp.exp(
        -rate_lane * (float(CHUNK) * lax.broadcasted_iota(jnp.int32, (count, lanes), 0).astype(F32))
    )
    power = jnp.concatenate([jnp.where(own, power[k:k + 1], 0.0) for k in range(count)], axis=0)
    power2 = jnp.concatenate(two_terms(power), axis=1)
    decays = [jnp.exp(-rate_lane * float(local_len * step)) for step in range(n_ctx - 1)]
    for name in ("residual", "gate", "gain"):
        loads[name].wait()
    gate = stack_chunks(gate_ref[...].astype(F32), count)
    base = stack_chunks(residual_ref[...], count) + gate * near
    gain = column_of(gain_ref, channels)

    pl.semaphore_wait(barrier, n_ctx - 1 - ctx + n_chan - 1)
    state_copies = {}
    for step in range(n_ctx - 1, 0, -1):
        copy = pltpu.make_async_remote_copy(
            src_ref=state_out,
            dst_ref=state_in.at[step - 1],
            send_sem=state_send.at[step - 1],
            recv_sem=state_recv.at[step - 1],
            device_id={"ctx": lax.rem(ctx + step, n_ctx)},
            device_id_type=MESH,
        )
        pl.when(ctx + step < n_ctx)(copy.start)
        state_copies[step] = copy

    carry_ref[...] = jnp.zeros((1, lanes), F32)
    for step in range(1, n_ctx):
        @pl.when(ctx >= step)
        def _():
            state_copies[step].wait_recv()
            carry_ref[...] += decays[step - 1] * state_in[step - 1]
    carry = carry_ref[...]
    arrive2 = jnp.concatenate(two_terms(leave * carry), axis=0)
    far = lax.dot_general(
        power2, jnp.concatenate([arrive2, arrive2], axis=1), (((1,), (1,)), ((), ())),
        preferred_element_type=F32,
    )
    added = gate * (far[:, :CHUNK] + far[:, CHUNK:])
    mixed = base + added
    square_out[...] = jnp.sum((mixed * mixed).reshape(count, channels, CHUNK), axis=1)

    square_copies = []
    for step in range(1, n_chan):
        copy = pltpu.make_async_remote_copy(
            src_ref=square_out,
            dst_ref=square_in.at[step - 1],
            send_sem=square_send.at[step - 1],
            recv_sem=square_recv.at[step - 1],
            device_id={"chan": lax.rem(chan + step, n_chan)},
            device_id_type=MESH,
        )
        copy.start()
        square_copies.append(copy)
    for k in range(count):
        tokens = slice(k * CHUNK, (k + 1) * CHUNK)
        base_out[:, tokens] = base[k * channels:(k + 1) * channels]
        added_out[:, tokens] = added[k * channels:(k + 1) * channels]
    for step in range(1, n_ctx):
        pl.when(ctx + step < n_ctx)(state_copies[step].wait_send)
    total = square_out[...]
    for step in range(1, n_chan):
        square_copies[step - 1].wait_recv()
        total = total + square_in[step - 1]
    scale = lax.rsqrt(total / float(channels * n_chan) + 1e-06)
    for k in range(count):
        scale_out[:, k * CHUNK:(k + 1) * CHUNK] = gain * scale[k:k + 1]
    for step in range(1, n_chan):
        square_copies[step - 1].wait_send()


def local(n_ctx, n_chan, value, gate, residual, rates, residues, skip, gain):
    channels, local_len = value.shape
    lanes = channels * rates.shape[1]
    count = local_len // CHUNK
    vmem = pl.BlockSpec(memory_space=pltpu.VMEM)
    hbm = pl.BlockSpec(memory_space=pltpu.HBM)
    base, added, scale = pl.pallas_call(
        functools.partial(kernel, n_ctx, n_chan),
        out_shape=(
            jax.ShapeDtypeStruct((channels, local_len), F32),
            jax.ShapeDtypeStruct((channels, local_len), F32),
            jax.ShapeDtypeStruct((channels, local_len), F32),
        ),
        in_specs=[hbm] * 7,
        out_specs=(vmem, vmem, vmem),
        scratch_shapes=[
            pltpu.VMEM(rates.shape, F32),
            pltpu.VMEM(residues.shape, F32),
            pltpu.VMEM(value.shape, BF16),
            pltpu.SMEM(skip.shape, F32),
            pltpu.VMEM(residual.shape, F32),
            pltpu.VMEM(gate.shape, BF16),
            pltpu.SMEM(gain.shape, F32),
            pltpu.SemaphoreType.DMA((7,)),
            pltpu.VMEM((1, lanes), F32),
            pltpu.VMEM((1, lanes), F32),
            pltpu.VMEM((n_ctx - 1, 1, lanes), F32),
            pltpu.VMEM((count, CHUNK), F32),
            pltpu.VMEM((n_chan - 1, count, CHUNK), F32),
            pltpu.SemaphoreType.DMA((n_ctx - 1,)),
            pltpu.SemaphoreType.DMA((n_ctx - 1,)),
            pltpu.SemaphoreType.DMA((n_chan - 1,)),
            pltpu.SemaphoreType.DMA((n_chan - 1,)),
        ],
        compiler_params=pltpu.CompilerParams(
            collective_id=0, has_side_effects=True, vmem_limit_bytes=32 * 1024 * 1024
        ),
        cost_estimate=pl.CostEstimate(
            flops=2 * count * channels * CHUNK * 2 * (channels * CHUNK + 3 * lanes),
            bytes_accessed=14 * channels * local_len,
            transcendentals=64 * 1024,
        ),
    )(*[
        pltpu.with_memory_space_constraint(x, pltpu.HBM)
        for x in (value, gate, residual, rates, residues, skip, gain)
    ])
    mixed = base + added
    return mixed, (mixed * scale).astype(BF16)


def solution(mesh):
    return jax.shard_map(
        functools.partial(local, mesh.shape["ctx"], mesh.shape["chan"]),
        mesh=mesh,
        in_specs=(
            P("chan", "ctx"),
            P("chan", "ctx"),
            P("chan", "ctx"),
            P("chan", None),
            P("chan", None),
            P("chan"),
            P("chan"),
        ),
        out_specs=(P("chan", "ctx"), P("chan", "ctx")),
        check_vma=False,
    )
```

```python
import functools

import jax
import jax.numpy as jnp
from jax import lax
from jax.experimental import pallas as pl
from jax.experimental.pallas import tpu as pltpu
from jax.sharding import PartitionSpec as P

CHUNK = 128
F32 = jnp.float32
BF16 = jnp.bfloat16
MESH = pl.DeviceIdType.MESH


def two_terms(x):
    high = x.astype(BF16)
    return high, (x - high.astype(F32)).astype(BF16)


def stack_chunks(x, count):
    return jnp.concatenate([x[:, k * CHUNK:(k + 1) * CHUNK] for k in range(count)], axis=0)


def column_of(ref, count):
    row = lax.broadcasted_iota(jnp.int32, (count, CHUNK), 0)
    out = jnp.zeros((count, CHUNK), F32)
    for c in range(count):
        out = jnp.where(row == c, ref[c], out)
    return out


def kernel(
    n_ctx, n_chan,
    value_hbm, gate_hbm, residual_hbm, rates_hbm, residues_hbm, skip_hbm, gain_hbm,
    base_out, added_out, scale_out,
    rates_ref, residues_ref, value_ref, skip_ref, residual_ref, gate_ref, gain_ref, load_sem,
    carry_ref, state_out, state_in, square_out, square_in,
    state_send, state_recv, square_send, square_recv,
):
    ctx = lax.axis_index("ctx")
    chan = lax.axis_index("chan")
    channels, local_len = value_ref.shape
    modes = rates_ref.shape[1]
    lanes = channels * modes
    count = local_len // CHUNK

    barrier = pltpu.get_barrier_semaphore()
    for step in range(n_ctx - 1, 0, -1):
        @pl.when(ctx >= step)
        def _():
            pl.semaphore_signal(
                barrier, inc=1, device_id={"ctx": lax.rem(ctx - step + n_ctx, n_ctx)}, device_id_type=MESH
            )
    for step in range(1, n_chan):
        pl.semaphore_signal(
            barrier, inc=1, device_id={"chan": lax.rem(chan + step, n_chan)}, device_id_type=MESH
        )

    loads = {}
    for order, (name, source, target) in enumerate([
        ("rates", rates_hbm, rates_ref),
        ("residues", residues_hbm, residues_ref),
        ("value", value_hbm, value_ref),
        ("skip", skip_hbm, skip_ref),
        ("residual", residual_hbm, residual_ref),
        ("gate", gate_hbm, gate_ref),
        ("gain", gain_hbm, gain_ref),
    ]):
        loads[name] = pltpu.make_async_copy(source, target, load_sem.at[order])
        loads[name].start()

    loads["rates"].wait()
    loads["residues"].wait()
    rates = rates_ref[...]
    weights = residues_ref[...] * jnp.sqrt(2.0 * rates)
    row8 = lax.broadcasted_iota(jnp.int32, (channels, lanes), 0)
    lane8 = lax.broadcasted_iota(jnp.int32, (channels, lanes), 1)
    token = lax.broadcasted_iota(jnp.int32, (channels, CHUNK), 1)
    time = token.astype(F32)
    taps = jnp.zeros((channels, CHUNK), F32)
    rate_rows = jnp.zeros((channels, lanes), F32)
    weight_rows = jnp.zeros((channels, lanes), F32)
    for m in range(modes):
        rate = jnp.broadcast_to(rates[:, m:m + 1], (channels, CHUNK))
        weight = jnp.broadcast_to(weights[:, m:m + 1], (channels, CHUNK))
        taps = taps + weight * jnp.exp(-rate * time)
        here = lane8 % modes == m
        rate_rows = jnp.where(here, rate, rate_rows)
        weight_rows = jnp.where(here, weight, weight_rows)
    own = row8 == lane8 // modes
    rate_lane = jnp.sum(jnp.where(own, rate_rows, 0.0), axis=0, keepdims=True)
    weight_lane = jnp.sum(jnp.where(own, weight_rows, 0.0), axis=0, keepdims=True)

    loads["value"].wait()
    signal = stack_chunks(value_ref[...].astype(F32), count)
    signal16 = signal.astype(BF16)
    place = lax.broadcasted_iota(jnp.int32, (CHUNK, lanes), 0).astype(F32)
    enter = jnp.exp(-rate_lane * (CHUNK - 1.0 - place))
    enter2 = jnp.concatenate(two_terms(enter), axis=1)
    added = jnp.dot(signal16, enter2, preferred_element_type=F32)
    added = added[:, :lanes] + added[:, lanes:]
    chunk_decay = jnp.exp(-rate_lane * float(CHUNK))
    state = jnp.zeros((channels, lanes), F32)
    states = []
    for k in range(count):
        states.append(state)
        chunk = jnp.where(own, added[k * channels:(k + 1) * channels], 0.0)
        state = chunk_decay * state + chunk
    state_out[...] = jnp.sum(state, axis=0, keepdims=True)

    loads["skip"].wait()
    taps = taps + jnp.where(token == 0, column_of(skip_ref, channels), 0.0)
    target = lax.broadcasted_iota(jnp.int32, (CHUNK, CHUNK), 1)
    source = lax.broadcasted_iota(jnp.int32, (CHUNK, CHUNK), 0)
    channel_of = lax.broadcasted_iota(jnp.int32, (count * channels, CHUNK), 0) % channels
    left, right = [], []
    for c in range(channels):
        wide = jnp.broadcast_to(taps[c:c + 1], (CHUNK, CHUNK))
        turned = pltpu.roll(wide, 0, 1, stride=1, stride_axis=0)
        toeplitz = jnp.where(target >= source, turned, 0.0)
        right.append(jnp.concatenate(two_terms(toeplitz), axis=1))
        left.append(jnp.where(channel_of == c, signal, 0.0).astype(BF16))
    close = jnp.dot(
        jnp.concatenate(left, axis=1), jnp.concatenate(right, axis=0), preferred_element_type=F32
    )
    leave = weight_lane * jnp.exp(-rate_lane * (place + 1.0))
    leave2 = jnp.concatenate(two_terms(leave), axis=0)
    leave2 = jnp.concatenate([leave2, leave2], axis=1)
    inside = lax.dot_general(
        jnp.concatenate(two_terms(jnp.concatenate(states, axis=0)), axis=1), leave2,
        (((1,), (1,)), ((), ())), preferred_element_type=F32,
    )
    near = close + inside
    near = near[:, :CHUNK] + near[:, CHUNK:]
    power = jnp.exp(
        -rate_lane * (float(CHUNK) * lax.broadcasted_iota(jnp.int32, (count, lanes), 0).astype(F32))
    )
    power = jnp.concatenate([jnp.where(own, power[k:k + 1], 0.0) for k in range(count)], axis=0)
    power2 = jnp.concatenate(two_terms(power), axis=1)
    decays = [jnp.exp(-rate_lane * float(local_len * step)) for step in range(n_ctx - 1)]
    for name in ("residual", "gate", "gain"):
        loads[name].wait()
    gate = stack_chunks(gate_ref[...].astype(F32), count)
    base = stack_chunks(residual_ref[...], count) + gate * near
    gain = column_of(gain_ref, channels)

    pl.semaphore_wait(barrier, n_ctx - 1 - ctx + n_chan - 1)
    state_copies = {}
    for step in range(n_ctx - 1, 0, -1):
        copy = pltpu.make_async_remote_copy(
            src_ref=state_out,
            dst_ref=state_in.at[step - 1],
            send_sem=state_send.at[step - 1],
            recv_sem=state_recv.at[step - 1],
            device_id={"ctx": lax.rem(ctx + step, n_ctx)},
            device_id_type=MESH,
        )
        pl.when(ctx + step < n_ctx)(copy.start)
        state_copies[step] = copy

    carry_ref[...] = jnp.zeros((1, lanes), F32)
    for step in range(1, n_ctx):
        @pl.when(ctx >= step)
        def _():
            state_copies[step].wait_recv()
            carry_ref[...] += decays[step - 1] * state_in[step - 1]
    carry = carry_ref[...]
    arrive2 = jnp.concatenate(two_terms(leave * carry), axis=0)
    far = lax.dot_general(
        power2, jnp.concatenate([arrive2, arrive2], axis=1), (((1,), (1,)), ((), ())),
        preferred_element_type=F32,
    )
    added = gate * (far[:, :CHUNK] + far[:, CHUNK:])
    mixed = base + added
    square_out[...] = jnp.sum((mixed * mixed).reshape(count, channels, CHUNK), axis=1)

    square_copies = {}
    order = sorted(range(1, n_chan), key=lambda step: -min(step, n_chan - step))
    for step in order:
        copy = pltpu.make_async_remote_copy(
            src_ref=square_out,
            dst_ref=square_in.at[step - 1],
            send_sem=square_send.at[step - 1],
            recv_sem=square_recv.at[step - 1],
            device_id={"chan": lax.rem(chan + step, n_chan)},
            device_id_type=MESH,
        )
        copy.start()
        square_copies[step] = copy
    for k in range(count):
        tokens = slice(k * CHUNK, (k + 1) * CHUNK)
        base_out[:, tokens] = base[k * channels:(k + 1) * channels]
        added_out[:, tokens] = added[k * channels:(k + 1) * channels]
    for step in range(1, n_ctx):
        pl.when(ctx + step < n_ctx)(state_copies[step].wait_send)
    total = square_out[...]
    for step in range(1, n_chan):
        square_copies[step].wait_recv()
        total = total + square_in[step - 1]
    scale = lax.rsqrt(total / float(channels * n_chan) + 1e-06)
    for k in range(count):
        scale_out[:, k * CHUNK:(k + 1) * CHUNK] = gain * scale[k:k + 1]
    for step in range(1, n_chan):
        square_copies[step].wait_send()


def local(n_ctx, n_chan, value, gate, residual, rates, residues, skip, gain):
    channels, local_len = value.shape
    lanes = channels * rates.shape[1]
    count = local_len // CHUNK
    vmem = pl.BlockSpec(memory_space=pltpu.VMEM)
    hbm = pl.BlockSpec(memory_space=pltpu.HBM)
    base, added, scale = pl.pallas_call(
        functools.partial(kernel, n_ctx, n_chan),
        out_shape=(
            jax.ShapeDtypeStruct((channels, local_len), F32),
            jax.ShapeDtypeStruct((channels, local_len), F32),
            jax.ShapeDtypeStruct((channels, local_len), F32),
        ),
        in_specs=[hbm] * 7,
        out_specs=(vmem, vmem, vmem),
        scratch_shapes=[
            pltpu.VMEM(rates.shape, F32),
            pltpu.VMEM(residues.shape, F32),
            pltpu.VMEM(value.shape, BF16),
            pltpu.SMEM(skip.shape, F32),
            pltpu.VMEM(residual.shape, F32),
            pltpu.VMEM(gate.shape, BF16),
            pltpu.SMEM(gain.shape, F32),
            pltpu.SemaphoreType.DMA((7,)),
            pltpu.VMEM((1, lanes), F32),
            pltpu.VMEM((1, lanes), F32),
            pltpu.VMEM((n_ctx - 1, 1, lanes), F32),
            pltpu.VMEM((count, CHUNK), F32),
            pltpu.VMEM((n_chan - 1, count, CHUNK), F32),
            pltpu.SemaphoreType.DMA((n_ctx - 1,)),
            pltpu.SemaphoreType.DMA((n_ctx - 1,)),
            pltpu.SemaphoreType.DMA((n_chan - 1,)),
            pltpu.SemaphoreType.DMA((n_chan - 1,)),
        ],
        compiler_params=pltpu.CompilerParams(
            collective_id=0, has_side_effects=True, vmem_limit_bytes=32 * 1024 * 1024
        ),
        cost_estimate=pl.CostEstimate(
            flops=2 * count * channels * CHUNK * 2 * (channels * CHUNK + 3 * lanes),
            bytes_accessed=14 * channels * local_len,
            transcendentals=64 * 1024,
        ),
    )(*[
        pltpu.with_memory_space_constraint(x, pltpu.HBM)
        for x in (value, gate, residual, rates, residues, skip, gain)
    ])
    mixed = base + added
    return mixed, (mixed * scale).astype(BF16)


def solution(mesh):
    return jax.shard_map(
        functools.partial(local, mesh.shape["ctx"], mesh.shape["chan"]),
        mesh=mesh,
        in_specs=(
            P("chan", "ctx"),
            P("chan", "ctx"),
            P("chan", "ctx"),
            P("chan", None),
            P("chan", None),
            P("chan"),
            P("chan"),
        ),
        out_specs=(P("chan", "ctx"), P("chan", "ctx")),
        check_vma=False,
    )
```

```python
import functools

import jax
import jax.numpy as jnp
from jax import lax
from jax.experimental import pallas as pl
from jax.experimental.pallas import tpu as pltpu
from jax.sharding import PartitionSpec as P

CHUNK = 128
F32 = jnp.float32
BF16 = jnp.bfloat16
MESH = pl.DeviceIdType.MESH


def two_terms(x):
    high = x.astype(BF16)
    return high, (x - high.astype(F32)).astype(BF16)


def stack_chunks(x, count):
    return jnp.concatenate([x[:, k * CHUNK:(k + 1) * CHUNK] for k in range(count)], axis=0)


def column_of(ref, count):
    row = lax.broadcasted_iota(jnp.int32, (count, CHUNK), 0)
    out = jnp.zeros((count, CHUNK), F32)
    for c in range(count):
        out = jnp.where(row == c, ref[c], out)
    return out


def kernel(
    n_ctx, n_chan,
    value_hbm, gate_hbm, residual_hbm, rates_hbm, residues_hbm, skip_hbm, gain_hbm,
    base_out, added_out, scale_out,
    rates_ref, residues_ref, value_ref, skip_ref, residual_ref, gate_ref, gain_ref, load_sem,
    carry_ref, state_out, state_in, square_out, square_in,
    state_send, state_recv, square_send, square_recv,
):
    ctx = lax.axis_index("ctx")
    chan = lax.axis_index("chan")
    channels, local_len = value_ref.shape
    modes = rates_ref.shape[1]
    lanes = channels * modes
    count = local_len // CHUNK

    barrier = pltpu.get_barrier_semaphore()
    for step in range(n_ctx - 1, 0, -1):
        @pl.when(ctx >= step)
        def _():
            pl.semaphore_signal(
                barrier, inc=1, device_id={"ctx": lax.rem(ctx - step + n_ctx, n_ctx)}, device_id_type=MESH
            )
    for step in range(1, n_chan):
        pl.semaphore_signal(
            barrier, inc=1, device_id={"chan": lax.rem(chan + step, n_chan)}, device_id_type=MESH
        )

    loads = {}
    for order, (name, source, target) in enumerate([
        ("rates", rates_hbm, rates_ref),
        ("residues", residues_hbm, residues_ref),
        ("value", value_hbm, value_ref),
        ("skip", skip_hbm, skip_ref),
        ("residual", residual_hbm, residual_ref),
        ("gate", gate_hbm, gate_ref),
        ("gain", gain_hbm, gain_ref),
    ]):
        loads[name] = pltpu.make_async_copy(source, target, load_sem.at[order])
        loads[name].start()

    loads["rates"].wait()
    loads["residues"].wait()
    rates = rates_ref[...]
    weights = residues_ref[...] * jnp.sqrt(2.0 * rates)
    row8 = lax.broadcasted_iota(jnp.int32, (channels, lanes), 0)
    lane8 = lax.broadcasted_iota(jnp.int32, (channels, lanes), 1)
    token = lax.broadcasted_iota(jnp.int32, (channels, CHUNK), 1)
    time = token.astype(F32)
    taps = jnp.zeros((channels, CHUNK), F32)
    rate_rows = jnp.zeros((channels, lanes), F32)
    weight_rows = jnp.zeros((channels, lanes), F32)
    for m in range(modes):
        rate = jnp.broadcast_to(rates[:, m:m + 1], (channels, CHUNK))
        weight = jnp.broadcast_to(weights[:, m:m + 1], (channels, CHUNK))
        taps = taps + weight * jnp.exp(-rate * time)
        here = lane8 % modes == m
        rate_rows = jnp.where(here, rate, rate_rows)
        weight_rows = jnp.where(here, weight, weight_rows)
    own = row8 == lane8 // modes
    rate_lane = jnp.sum(jnp.where(own, rate_rows, 0.0), axis=0, keepdims=True)
    weight_lane = jnp.sum(jnp.where(own, weight_rows, 0.0), axis=0, keepdims=True)

    loads["value"].wait()
    signal = stack_chunks(value_ref[...].astype(F32), count)
    signal16 = signal.astype(BF16)
    place = lax.broadcasted_iota(jnp.int32, (CHUNK, lanes), 0).astype(F32)
    enter = jnp.exp(-rate_lane * (CHUNK - 1.0 - place))
    enter2 = jnp.concatenate(two_terms(enter), axis=1)
    added = jnp.dot(signal16, enter2, preferred_element_type=F32)
    added = added[:, :lanes] + added[:, lanes:]
    chunk_decay = jnp.exp(-rate_lane * float(CHUNK))
    state = jnp.zeros((channels, lanes), F32)
    states = []
    for k in range(count):
        states.append(state)
        chunk = jnp.where(own, added[k * channels:(k + 1) * channels], 0.0)
        state = chunk_decay * state + chunk
    state_out[...] = jnp.sum(state, axis=0, keepdims=True)

    loads["skip"].wait()
    taps = taps + jnp.where(token == 0, column_of(skip_ref, channels), 0.0)
    target = lax.broadcasted_iota(jnp.int32, (CHUNK, CHUNK), 1)
    source = lax.broadcasted_iota(jnp.int32, (CHUNK, CHUNK), 0)
    channel_of = lax.broadcasted_iota(jnp.int32, (count * channels, CHUNK), 0) % channels
    left, right = [], []
    for c in range(channels):
        wide = jnp.broadcast_to(taps[c:c + 1], (CHUNK, CHUNK))
        turned = pltpu.roll(wide, 0, 1, stride=1, stride_axis=0)
        toeplitz = jnp.where(target >= source, turned, 0.0)
        right.append(jnp.concatenate(two_terms(toeplitz), axis=1))
        left.append(jnp.where(channel_of == c, signal, 0.0).astype(BF16))
    close = jnp.dot(
        jnp.concatenate(left, axis=1), jnp.concatenate(right, axis=0), preferred_element_type=F32
    )
    leave = weight_lane * jnp.exp(-rate_lane * (place + 1.0))
    leave2 = jnp.concatenate(two_terms(leave), axis=0)
    leave2 = jnp.concatenate([leave2, leave2], axis=1)
    inside = lax.dot_general(
        jnp.concatenate(two_terms(jnp.concatenate(states, axis=0)), axis=1), leave2,
        (((1,), (1,)), ((), ())), preferred_element_type=F32,
    )
    near = close + inside
    near = near[:, :CHUNK] + near[:, CHUNK:]
    power = jnp.exp(
        -rate_lane * (float(CHUNK) * lax.broadcasted_iota(jnp.int32, (count, lanes), 0).astype(F32))
    )
    power = jnp.concatenate([jnp.where(own, power[k:k + 1], 0.0) for k in range(count)], axis=0)
    turned2 = jnp.concatenate(two_terms(leave.T), axis=1)
    turned2 = jnp.concatenate([turned2, turned2], axis=0)
    decays = [jnp.exp(-rate_lane * float(local_len * step)) for step in range(n_ctx - 1)]
    for name in ("residual", "gate", "gain"):
        loads[name].wait()
    gate = stack_chunks(gate_ref[...].astype(F32), count)
    base = stack_chunks(residual_ref[...], count) + gate * near
    gain = column_of(gain_ref, channels)

    pl.semaphore_wait(barrier, n_ctx - 1 - ctx + n_chan - 1)
    state_copies = {}
    for step in range(n_ctx - 1, 0, -1):
        copy = pltpu.make_async_remote_copy(
            src_ref=state_out,
            dst_ref=state_in.at[step - 1],
            send_sem=state_send.at[step - 1],
            recv_sem=state_recv.at[step - 1],
            device_id={"ctx": lax.rem(ctx + step, n_ctx)},
            device_id_type=MESH,
        )
        pl.when(ctx + step < n_ctx)(copy.start)
        state_copies[step] = copy

    carry_ref[...] = jnp.zeros((1, lanes), F32)
    for step in range(1, n_ctx):
        @pl.when(ctx >= step)
        def _():
            state_copies[step].wait_recv()
            carry_ref[...] += decays[step - 1] * state_in[step - 1]
    carry = carry_ref[...]
    arrive2 = jnp.concatenate(two_terms(power * carry), axis=1)
    far = jnp.dot(arrive2, turned2, preferred_element_type=F32)
    added = gate * (far[:, :CHUNK] + far[:, CHUNK:])
    mixed = base + added
    square_out[...] = jnp.sum((mixed * mixed).reshape(count, channels, CHUNK), axis=1)

    square_copies = {}
    order = sorted(range(1, n_chan), key=lambda step: -min(step, n_chan - step))
    for step in order:
        copy = pltpu.make_async_remote_copy(
            src_ref=square_out,
            dst_ref=square_in.at[step - 1],
            send_sem=square_send.at[step - 1],
            recv_sem=square_recv.at[step - 1],
            device_id={"chan": lax.rem(chan + step, n_chan)},
            device_id_type=MESH,
        )
        copy.start()
        square_copies[step] = copy
    for k in range(count):
        tokens = slice(k * CHUNK, (k + 1) * CHUNK)
        base_out[:, tokens] = base[k * channels:(k + 1) * channels]
        added_out[:, tokens] = added[k * channels:(k + 1) * channels]
    for step in range(1, n_ctx):
        pl.when(ctx + step < n_ctx)(state_copies[step].wait_send)
    total = square_out[...]
    for step in range(1, n_chan):
        square_copies[step].wait_recv()
        total = total + square_in[step - 1]
    scale = lax.rsqrt(total / float(channels * n_chan) + 1e-06)
    for k in range(count):
        scale_out[:, k * CHUNK:(k + 1) * CHUNK] = gain * scale[k:k + 1]
    for step in range(1, n_chan):
        square_copies[step].wait_send()


def local(n_ctx, n_chan, value, gate, residual, rates, residues, skip, gain):
    channels, local_len = value.shape
    lanes = channels * rates.shape[1]
    count = local_len // CHUNK
    vmem = pl.BlockSpec(memory_space=pltpu.VMEM)
    hbm = pl.BlockSpec(memory_space=pltpu.HBM)
    base, added, scale = pl.pallas_call(
        functools.partial(kernel, n_ctx, n_chan),
        out_shape=(
            jax.ShapeDtypeStruct((channels, local_len), F32),
            jax.ShapeDtypeStruct((channels, local_len), F32),
            jax.ShapeDtypeStruct((channels, local_len), F32),
        ),
        in_specs=[hbm] * 7,
        out_specs=(vmem, vmem, vmem),
        scratch_shapes=[
            pltpu.VMEM(rates.shape, F32),
            pltpu.VMEM(residues.shape, F32),
            pltpu.VMEM(value.shape, BF16),
            pltpu.SMEM(skip.shape, F32),
            pltpu.VMEM(residual.shape, F32),
            pltpu.VMEM(gate.shape, BF16),
            pltpu.SMEM(gain.shape, F32),
            pltpu.SemaphoreType.DMA((7,)),
            pltpu.VMEM((1, lanes), F32),
            pltpu.VMEM((1, lanes), F32),
            pltpu.VMEM((n_ctx - 1, 1, lanes), F32),
            pltpu.VMEM((count, CHUNK), F32),
            pltpu.VMEM((n_chan - 1, count, CHUNK), F32),
            pltpu.SemaphoreType.DMA((n_ctx - 1,)),
            pltpu.SemaphoreType.DMA((n_ctx - 1,)),
            pltpu.SemaphoreType.DMA((n_chan - 1,)),
            pltpu.SemaphoreType.DMA((n_chan - 1,)),
        ],
        compiler_params=pltpu.CompilerParams(
            collective_id=0, has_side_effects=True, vmem_limit_bytes=32 * 1024 * 1024
        ),
        cost_estimate=pl.CostEstimate(
            flops=2 * count * channels * CHUNK * 2 * (channels * CHUNK + 3 * lanes),
            bytes_accessed=14 * channels * local_len,
            transcendentals=64 * 1024,
        ),
    )(*[
        pltpu.with_memory_space_constraint(x, pltpu.HBM)
        for x in (value, gate, residual, rates, residues, skip, gain)
    ])
    mixed = base + added
    return mixed, (mixed * scale).astype(BF16)


def solution(mesh):
    return jax.shard_map(
        functools.partial(local, mesh.shape["ctx"], mesh.shape["chan"]),
        mesh=mesh,
        in_specs=(
            P("chan", "ctx"),
            P("chan", "ctx"),
            P("chan", "ctx"),
            P("chan", None),
            P("chan", None),
            P("chan"),
            P("chan"),
        ),
        out_specs=(P("chan", "ctx"), P("chan", "ctx")),
        check_vma=False,
    )
```
